1024 devices in a mesh: grp: 16 (over x, z_hi), inner: 64 (over y, z_lo, core).
Axes of the slice: x: 4, y: 4, z: 32 (z_hi: 4, z_lo: 8; z = z_hi * 8 + z_lo), core: 2. Of those that a mesh axis runs over, the one named last changes fastest.
Arguments:
- tokens: bfloat16 [131072, 4096], P(('grp', 'inner')), may hold values from -24 to 24
- norm_gain: float32 [4096], replicated, may hold values from 0.1 to 1.9
- key_weight: bfloat16 [4096, 512], P('inner'), may hold values from -0.09375 to 0.09375
- key_grad: bfloat16 [131072, 512], P(('grp', 'inner')), may hold values from -6 to 6
Outputs:
- keys: bfloat16 [131072, 512], P(('grp', 'inner'))
- input_grad: bfloat16 [131072, 4096], P(('grp', 'inner'))
- weight_grad: float32 [4096, 512], P(('grp', 'inner'))
The draws below stay inside these ranges and needn't reach their ends.
All inputs are finite; a program needn't handle non-finite values.
Results may differ from the reference program's by a relative error of at most 0.015.
Values may be sent and summed in bfloat16 or wider, within the bound.
A program may use at most 64 MiB of HBM per device.

```python
import jax
import jax.numpy as jnp
from jax import lax

D = 4096
TOK_DEV = 128
KW = 512
TOKENS = 131072


def strengthened(entries, own_key, source, target, parts, factor):
    def block_of(position):
        return (jnp.arange(entries.shape[position]) // (entries.shape[position] // parts)).reshape((-1,) + (1,) * (entries.ndim - 1 - position))

    first = jax.random.permutation(own_key, parts)[block_of(target)]
    far = (block_of(target) + parts // 2) % parts
    return jnp.where((block_of(source) == first) | (block_of(source) == far), factor * entries, entries)


def shard_levels(key, shape, split, smallest, top_value):
    loudness = 1.0
    for dim, blocks in split:
        draws = jax.random.uniform(jax.random.fold_in(jax.random.fold_in(key, 6), dim), (blocks,), jnp.float32, smallest / len(split), top_value / len(split))
        loudness = loudness * jnp.repeat(jnp.exp(draws), shape[dim] // blocks).reshape((-1,) + (1,) * (len(shape) - 1 - dim))
    return loudness


def gaussian(stream_key, extent, spread, bound, cuts=(), held_as=jnp.bfloat16):
    gain = shard_levels(stream_key, extent, cuts, -0.22, 0.18) if cuts else 1.0
    result = jax.random.normal(stream_key, extent, jnp.float32) * spread * gain
    return jnp.minimum(jnp.maximum(result, -bound), bound).astype(held_as)


def noise_with(rng, dims, spread, bound, pieces, heavy, held_as=jnp.bfloat16):
    values = spread * jax.random.normal(rng, dims, jnp.float32)
    if pieces:
        values = values * shard_levels(rng, dims, pieces, -0.22, 0.18)
    return jnp.clip(strengthened(values, jax.random.fold_in(rng, 3), *heavy), -bound, bound).astype(held_as)


def setup_inputs(seed: int = 0) -> dict:
    key_of = jax.random.split(jax.random.key(seed), 5)
    tokens = noise_with(key_of[0], (TOKENS, D), 1.0, 24.0, ((0, 1024),), (0, 1, 1024, 6.0))
    norm_gain = jnp.clip(1.0 + 0.18 * jax.random.normal(key_of[1], (D,), jnp.float32), 0.1, 1.9)
    key_weight = gaussian(key_of[2], (D, KW), D ** -0.5, 0.09375, ((0, 64),))
    key_grad = gaussian(key_of[3], (TOKENS, KW), 1.0, 6.0, ((0, 1024),))
    return dict(tokens=tokens, norm_gain=norm_gain, key_weight=key_weight, key_grad=key_grad)


def reference(tokens, norm_gain, key_weight, key_grad):
    values = tokens.astype(jnp.float32)
    inverse = lax.rsqrt(lax.optimization_barrier(jnp.mean(values * values, axis=-1, keepdims=True)) + 1e-05)
    unit = values * inverse
    normed = (unit * norm_gain).astype(jnp.bfloat16)
    keys = jnp.dot(normed, key_weight, preferred_element_type=jnp.float32).astype(jnp.bfloat16)
    normed_grad = jnp.dot(key_grad, key_weight.T, preferred_element_type=jnp.float32)
    scaled_grad = normed_grad * norm_gain
    centre = lax.optimization_barrier(jnp.mean(scaled_grad * unit, axis=-1, keepdims=True))
    input_grad = ((scaled_grad - unit * centre) * inverse).astype(jnp.bfloat16)
    blocks = TOKENS // TOK_DEV
    normed_blocks = normed.reshape(blocks, TOK_DEV, D)
    grad_blocks = key_grad.reshape(blocks, TOK_DEV, KW)

    def add_block(total, pair):
        block_term = jnp.dot(pair[0].T, pair[1], preferred_element_type=jnp.float32).astype(jnp.bfloat16)
        block_term = lax.optimization_barrier(block_term)
        return (total + block_term.astype(jnp.float32), None)
    summed, _ = lax.scan(add_block, jnp.zeros((D, KW), jnp.float32), (normed_blocks, grad_blocks))
    weight_grad = summed * TOKENS ** (-0.5)
    return (keys, input_grad, weight_grad)
```

```python
import functools

import jax
import jax.numpy as jnp
from jax import lax
from jax.experimental import pallas as pl
from jax.experimental.pallas import tpu as pltpu
from jax.sharding import PartitionSpec as P

TOK = 128
D = 4096
KW = 512
TOKENS = 131072
F32 = jnp.float32
BF16 = jnp.bfloat16
MESH = pl.DeviceIdType.MESH
WINDOW = (-4, -3, -2, -1, 1, 2, 3)
Z_PEERS = (1, 2, 3, 4, 8, 12, 16, 20, 24, 28, 29, 30, 31)


def kernel(
    tok_ref, gain_ref, w_ref, kg_ref, keys_ref, ig_ref, wg_ref,
    n2, kg2, inv, ta, tb, ra, rb, sa, sb, ra2, rb2, zbuf, rza, zb2, rzb,
    fsend, frecv, wbuf, sg, acc,
    swap_s, swap_r, gz_s, gz_r, a1_s, a1_r, b1_s, b1_r, a2_s, a2_r, b2_s, b2_r,
    za_s, za_r, zb_s, zb_r, g0p_s, g0p_r, g1p_s, g1p_r, g0q_s, g0q_r, g1q_s, g1q_r,
    fw_s, fw_r, fin_s, fin_r,
):
    grp = lax.axis_index("grp")
    inner = lax.axis_index("inner")
    x = grp // 4
    z = (grp % 4) * 8 + (inner // 2) % 8
    y = inner // 16
    c = inner % 2
    oc = 1 - c
    zl = z % 8
    zg = z // 4
    zm = z % 4

    def dev(px, py, pz, pc):
        return (px * 4 + pz // 8, (py * 8 + pz % 8) * 2 + pc)

    sends = []

    def send(src, dst, s, r, target):
        copy = pltpu.make_async_remote_copy(
            src_ref=src, dst_ref=dst, send_sem=s, recv_sem=r,
            device_id=target, device_id_type=MESH,
        )
        copy.start()
        sends.append(copy)
        return copy

    xp = [(x + k) % 4 for k in range(4)]
    yp = [(y + k) % 4 for k in range(4)]
    partner = dev(x, y, z, oc)

    barrier = pltpu.get_barrier_semaphore()
    peers = [partner]
    peers += [dev(xp[k], y, z, c) for k in (1, 2, 3)]
    peers += [dev(x, yp[k], z, c) for k in (1, 2, 3)]
    peers += [dev(x, y, (z + k) % 32, c) for k in Z_PEERS]
    for peer in peers:
        pl.semaphore_signal(barrier, inc=1, device_id=peer, device_id_type=MESH)

    total = jnp.zeros((TOK, 128), F32)
    for j in range(D // 512):
        v = tok_ref[:, j * 512:(j + 1) * 512].astype(F32)
        v = v * v
        for i in range(4):
            total = total + v[:, i * 128:(i + 1) * 128]
    inverse = lax.rsqrt(jnp.sum(total, axis=-1, keepdims=True) * (1.0 / D) + 1e-05)
    inv[...] = inverse
    for j in range(4):
        v = tok_ref[:, j * 1024:(j + 1) * 1024].astype(F32) * inverse
        n2[c, j] = (v * gain_ref[:, j * 1024:(j + 1) * 1024]).astype(BF16)
    kg2[c] = kg_ref[:, pl.ds(pl.multiple_of(c * 256, 256), 256)]
    wbuf[y, zl, c * 4 + x] = w_ref[pl.ds(pl.multiple_of(x * 16, 16), 16), :]

    pl.semaphore_wait(barrier, len(peers))

    kg_copy = send(
        kg_ref.at[:, pl.ds(pl.multiple_of(oc * 256, 256), 256)], kg2.at[c],
        swap_s.at[4], swap_r.at[4], partner,
    )
    order = (2, 1, 3, 0)
    swaps = {}
    for k in order:
        swaps[k] = send(n2.at[c, xp[k]], n2.at[c, xp[k]], swap_s.at[k], swap_r.at[k], partner)

    gz = []
    for n, k in enumerate(WINDOW):
        piece = wbuf.at[y, zl, c * 4 + x]
        gz.append(send(piece, piece, gz_s.at[n], gz_r.at[n], dev(x, y, (z + k) % 32, c)))

    kg_copy.wait_recv()
    a1, b1 = {}, {}
    for k in order:
        swaps[k].wait_recv()
        xt = xp[k]
        for j in range(4):
            lhs = n2[:, xt, :, j * 256:(j + 1) * 256].reshape(2 * TOK, 256)
            t = lax.dot_general(
                lhs, kg2[...].reshape(2 * TOK, 256), (((0,), (0,)), ((), ())),
                preferred_element_type=F32,
            ).astype(BF16)
            ta[xt, j] = t[:, :128].reshape(4, 64, 128)
            tb[xt, j] = t[:, 128:].reshape(4, 64, 128)
        if k:
            a1[k] = send(ta.at[xt], ra.at[k - 1], a1_s.at[k - 1], a1_r.at[k - 1], dev(xt, y, z, c))
    for k in (2, 1, 3):
        b1[k] = send(
            tb.at[:, :, yp[k]], rb.at[k - 1], b1_s.at[k - 1], b1_r.at[k - 1], dev(x, yp[k], z, c)
        )

    for copy in gz:
        copy.wait_recv()

    for k in (1, 3, 2):
        a1[k].wait_recv()
    for j in range(4):
        v = ta[x, j].astype(F32)
        for k in range(3):
            v = v + ra[k, j].astype(F32)
        sa[j] = v.astype(BF16)
    a2 = [
        send(sa.at[:, yp[k]], ra2.at[k - 1], a2_s.at[k - 1], a2_r.at[k - 1], dev(x, yp[k], z, c))
        for k in (2, 1, 3)
    ]
    for k in (1, 3, 2):
        b1[k].wait_recv()
    for j in range(4):
        v = tb[j, :, y].astype(F32)
        for k in range(3):
            v = v + rb[k, j].astype(F32)
        sb[j] = v.astype(BF16)
    b2 = [
        send(sb.at[xp[k]], rb2.at[k - 1], b2_s.at[k - 1], b2_r.at[k - 1], dev(xp[k], y, z, c))
        for k in (2, 1, 3)
    ]
    g0p = []
    g1p = []
    for k in (2, 1, 3):
        piece = wbuf.at[y, 0:4, c * 4 + x]
        g0p.append(send(piece, piece, g0p_s.at[k - 1], g0p_r.at[k - 1], dev(xp[k], y, z, c)))
        piece = wbuf.at[y, 4:8, c * 4 + x]
        g1p.append(send(piece, piece, g1p_s.at[k - 1], g1p_r.at[k - 1], dev(x, yp[k], z, c)))

    for copy in a2:
        copy.wait_recv()
    for copy in b2:
        copy.wait_recv()
    fa = sa[:, y].astype(F32)
    fb = sb[x].astype(F32)
    for k in range(3):
        fa = fa + ra2[k].astype(F32)
        fb = fb + rb2[k].astype(F32)
    both = jnp.concatenate([fa.reshape(8, 4, 8, 128), fb.reshape(8, 4, 8, 128)], axis=2)
    zbuf[...] = both.astype(BF16)
    za = [
        send(
            zbuf.at[:, (zm + k) % 4], rza.at[k - 1], za_s.at[k - 1], za_r.at[k - 1],
            dev(x, y, zg * 4 + (zm + k) % 4, c),
        )
        for k in (1, 2, 3)
    ]

    forwards = []

    def forward(piece):
        n = len(forwards)
        forwards.append(send(piece, piece, fw_s.at[n], fw_r.at[n], partner))

    for copy in g0p:
        copy.wait_recv()
    g0q = {}
    for k in (2, 1, 3):
        piece = wbuf.at[y, 0:4, pl.ds(c * 4, 4)]
        g0q[k] = send(piece, piece, g0q_s.at[k - 1], g0q_r.at[k - 1], dev(x, yp[k], z, c))
    for copy in g1p:
        copy.wait_recv()
    g1q = {}
    for k in (2, 1, 3):
        piece = wbuf.at[:, 4:8, c * 4 + x]
        g1q[k] = send(piece, piece, g1q_s.at[k - 1], g1q_r.at[k - 1], dev(xp[k], y, z, c))
    forward(wbuf.at[y, 0:4, pl.ds(c * 4, 4)])
    forward(wbuf.at[:, 4:8, c * 4 + x])

    for copy in za:
        copy.wait_recv()
    v = zbuf[:, zm].astype(F32)
    for k in range(3):
        v = v + rza[k].astype(F32)
    zb2[...] = v.astype(BF16)
    zb = []
    for k in (4, 3, 5, 2, 6, 1, 7):
        gt = (zg + k) % 8
        zb.append(
            send(zb2.at[gt], rzb.at[k - 1], zb_s.at[k - 1], zb_r.at[k - 1], dev(x, y, gt * 4 + zm, c))
        )

    for k in (1, 3, 2):
        g0q[k].wait_recv()
        forward(wbuf.at[yp[4 - k], 0:4, pl.ds(c * 4, 4)])
        g1q[k].wait_recv()
        forward(wbuf.at[:, 4:8, c * 4 + xp[4 - k]])

    for copy in zb:
        copy.wait_recv()
    v = zb2[zg].astype(F32)
    for k in range(7):
        v = v + rzb[k].astype(F32)
    v = v * (TOKENS ** -0.5)
    low = jnp.concatenate([v[0:4], v[8:12]], axis=0)
    high = jnp.concatenate([v[4:8], v[12:16]], axis=0)
    mine = jnp.where(c == 0, low, high)
    fsend[...] = jnp.where(c == 0, high, low)
    fin = send(fsend, frecv, fin_s.at[0], fin_r.at[0], partner)

    for copy in forwards:
        copy.wait_recv()
    acc[...] = jnp.zeros_like(acc)

    def block(j, dots):
        for i in range(4):
            rows = slice(i * 256, (i + 1) * 256)
            w = wbuf[j, i * 2:(i + 1) * 2].reshape(256, KW)
            normed = n2[c, j, :, rows]
            acc[...] += jnp.dot(normed, w, preferred_element_type=F32)
            cols = pl.ds(pl.multiple_of(j * 1024 + i * 256, 256), 256)
            ng = lax.dot_general(
                kg_ref[...], w, (((1,), (1,)), ((), ())), preferred_element_type=F32
            )
            s = ng * gain_ref[:, cols]
            sg[j, :, rows] = s
            p = s * (tok_ref[:, cols].astype(F32) * inv[...])
            dots = dots + p[:, :128] + p[:, 128:]
        return dots

    dots = lax.fori_loop(0, 4, block, jnp.zeros((TOK, 128), F32))
    keys_ref[...] = acc[...].astype(BF16)
    centre = jnp.sum(dots, axis=-1, keepdims=True) * (1.0 / D)

    def finish(j, carry):
        cols = pl.ds(pl.multiple_of(j * 1024, 1024), 1024)
        unit = tok_ref[:, cols].astype(F32) * inv[...]
        ig_ref[:, cols] = ((sg[j] - unit * centre) * inv[...]).astype(BF16)
        return carry

    lax.fori_loop(0, 4, finish, 0)

    fin.wait_recv()
    other = frecv[...]
    first = jnp.where(c == 0, mine, other)
    second = jnp.where(c == 0, other, mine)
    wg_ref[:, 0:128] = first[0:4]
    wg_ref[:, 128:256] = first[4:8]
    wg_ref[:, 256:384] = second[0:4]
    wg_ref[:, 384:512] = second[4:8]

    for copy in sends:
        copy.wait_send()


def shards(tokens, norm_gain, key_weight, key_grad):
    vmem = pl.BlockSpec(memory_space=pltpu.VMEM)
    pairs = (5, 7, 3, 3, 3, 3, 3, 7, 3, 3, 3, 3, 8, 1)
    sems = []
    for n in pairs:
        sems += [pltpu.SemaphoreType.DMA((n,)), pltpu.SemaphoreType.DMA((n,))]
    return pl.pallas_call(
        kernel,
        name="key_projection",
        out_shape=(
            jax.ShapeDtypeStruct((TOK, KW), BF16),
            jax.ShapeDtypeStruct((TOK, D), BF16),
            jax.ShapeDtypeStruct((4, KW), F32),
        ),
        in_specs=[vmem] * 4,
        out_specs=(vmem, vmem, vmem),
        scratch_shapes=[
            pltpu.VMEM((2, 4, TOK, 1024), BF16),
            pltpu.VMEM((2, TOK, 256), BF16),
            pltpu.VMEM((TOK, 1), F32),
            pltpu.VMEM((4, 4, 4, 64, 128), BF16),
            pltpu.VMEM((4, 4, 4, 64, 128), BF16),
            pltpu.VMEM((3, 4, 4, 64, 128), BF16),
            pltpu.VMEM((3, 4, 4, 64, 128), BF16),
            pltpu.VMEM((4, 4, 64, 128), BF16),
            pltpu.VMEM((4, 4, 64, 128), BF16),
            pltpu.VMEM((3, 4, 64, 128), BF16),
            pltpu.VMEM((3, 4, 64, 128), BF16),
            pltpu.VMEM((8, 4, 16, 128), BF16),
            pltpu.VMEM((3, 8, 16, 128), BF16),
            pltpu.VMEM((8, 16, 128), BF16),
            pltpu.VMEM((7, 16, 128), BF16),
            pltpu.VMEM((8, 128), F32),
            pltpu.VMEM((8, 128), F32),
            pltpu.VMEM((4, 8, 8, 16, KW), BF16),
            pltpu.VMEM((4, TOK, 1024), F32),
            pltpu.VMEM((TOK, KW), F32),
        ] + sems,
        compiler_params=pltpu.CompilerParams(
            collective_id=0, has_side_effects=True, vmem_limit_bytes=48 * 2**20
        ),
    )(tokens, norm_gain.reshape(1, D), key_weight, key_grad)


def solution(mesh):
    return jax.shard_map(
        shards,
        mesh=mesh,
        in_specs=(P(("grp", "inner"), None), P(), P("inner", None), P(("grp", "inner"), None)),
        out_specs=(P(("grp", "inner"), None), P(("grp", "inner"), None), P(("grp", "inner"), None)),
        check_vma=False,
    )
```

```python
import functools

import jax
import jax.numpy as jnp
from jax import lax
from jax.experimental import pallas as pl
from jax.experimental.pallas import tpu as pltpu
from jax.sharding import PartitionSpec as P

TOK = 128
D = 4096
KW = 512
TOKENS = 131072
F32 = jnp.float32
BF16 = jnp.bfloat16
MESH = pl.DeviceIdType.MESH
WINDOW = (-4, -3, -2, -1, 1, 2, 3)
Z_NEAR = (1, 2, 3, 4, 28, 29, 30, 31)


def kernel(
    tok_hbm, gain_hbm, w_hbm, kg_hbm, keys_ref, ig_ref, wg_ref,
    tok_ref, gain_ref, kg_ref, nrm, n2, kg2, inv, ta, tb, ra, rb, sa, sb, ra2, rb2, zbuf, rza, zb2, rzb,
    fsend, frecv, wbuf, sg, acc,
    swap_s, swap_r, gz_s, gz_r, a1_s, a1_r, b1_s, b1_r, a2_s, a2_r, b2_s, b2_r,
    za_s, za_r, zb_s, zb_r, g0p_s, g0p_r, g1p_s, g1p_r, g0q_s, g0q_r, g1q_s, g1q_r,
    fw_s, fw_r, fin_s, fin_r, load_s, far_s,
):
    grp = lax.axis_index("grp")
    inner = lax.axis_index("inner")
    x = grp // 4
    z = (grp % 4) * 8 + (inner // 2) % 8
    y = inner // 16
    c = inner % 2
    oc = 1 - c
    zl = z % 8
    zg = z // 4
    zm = z % 4

    def dev(px, py, pz, pc):
        return (px * 4 + pz // 8, (py * 8 + pz % 8) * 2 + pc)

    sends = []

    def send(src, dst, s, r, target):
        copy = pltpu.make_async_remote_copy(
            src_ref=src, dst_ref=dst, send_sem=s, recv_sem=r,
            device_id=target, device_id_type=MESH,
        )
        copy.start()
        sends.append(copy)
        return copy

    xp = [(x + k) % 4 for k in range(4)]
    yp = [(y + k) % 4 for k in range(4)]
    partner = dev(x, y, z, oc)

    barrier = pltpu.get_barrier_semaphore()
    peers = [partner]
    peers += [dev(xp[k], y, z, c) for k in (1, 2, 3)]
    peers += [dev(x, yp[k], z, c) for k in (1, 2, 3)]
    peers += [dev(x, y, (z + k) % 32, c) for k in Z_NEAR]
    for peer in peers:
        pl.semaphore_signal(barrier, inc=1, device_id=peer, device_id_type=MESH)

    w_own = w_hbm.at[pl.ds(pl.multiple_of(x * 16, 16), 16), :]
    loads = [
        pltpu.make_async_copy(src, dst, load_s.at[n])
        for n, (src, dst) in enumerate(
            (
                (tok_hbm, tok_ref), (gain_hbm, gain_ref), (kg_hbm, kg_ref),
                (w_own, wbuf.at[y, zl, c * 4 + x]),
            )
        )
    ]
    for copy in loads:
        copy.start()
    pl.semaphore_wait(barrier, len(peers))

    gz = []
    for n, k in enumerate(WINDOW):
        gz.append(
            send(
                w_own, wbuf.at[y, zl, c * 4 + x], gz_s.at[n], gz_r.at[n],
                dev(x, y, (z + k) % 32, c),
            )
        )

    for k in (4, 28):
        pl.semaphore_signal(
            far_s.at[0], inc=1, device_id=dev(x, y, (z + k) % 32, c), device_id_type=MESH
        )

    for copy in loads:
        copy.wait()
    kg_copy = send(
        kg_ref.at[:, pl.ds(pl.multiple_of(oc * 256, 256), 256)], kg2.at[c],
        swap_s.at[4], swap_r.at[4], partner,
    )
    kg2[c] = kg_ref[:, pl.ds(pl.multiple_of(c * 256, 256), 256)]
    total = jnp.zeros((TOK, 128), F32)
    for j in range(D // 512):
        v = tok_ref[:, j * 512:(j + 1) * 512].astype(F32)
        v = v * v
        for i in range(4):
            total = total + v[:, i * 128:(i + 1) * 128]
    inverse = lax.rsqrt(jnp.sum(total, axis=-1, keepdims=True) * (1.0 / D) + 1e-05)
    inv[...] = inverse
    order = (2, 1, 3, 0)
    swaps = {}
    for k in order:
        cols = pl.ds(pl.multiple_of(xp[k] * 1024, 1024), 1024)
        v = tok_ref[:, cols].astype(F32) * inverse
        v = (v * gain_ref[:, cols]).astype(BF16)
        nrm[xp[k]] = v
        n2[xp[k], c] = v.T
        piece = n2.at[xp[k], c]
        swaps[k] = send(piece, piece, swap_s.at[k], swap_r.at[k], partner)

    kg_copy.wait_recv()
    a1, b1 = {}, []
    for k in order:
        swaps[k].wait_recv()
        xt = xp[k]
        for j in range(4):
            rows = slice(j * 256, (j + 1) * 256)
            lhs = jnp.concatenate([n2[xt, 0, rows], n2[xt, 1, rows]], axis=1)
            t = jnp.dot(
                lhs, kg2[...].reshape(2 * TOK, 256), preferred_element_type=F32
            ).astype(BF16)
            ta[xt, j] = t[:, :128].reshape(4, 64, 128)
            tb[xt, j] = t[:, 128:].reshape(4, 64, 128)
        if k:
            a1[k] = send(ta.at[xt], ra.at[k - 1], a1_s.at[k - 1], a1_r.at[k - 1], dev(xt, y, z, c))
        for i in (2, 1, 3):
            n = k * 3 + i - 1
            b1.append(
                send(
                    tb.at[xt, :, yp[i]], rb.at[i - 1, (x + k) % 4], b1_s.at[n], b1_r.at[n],
                    dev(x, yp[i], z, c),
                )
            )
    pl.semaphore_wait(far_s.at[0], 2)
    for k in (8, 24):
        pl.semaphore_signal(
            far_s.at[1], inc=1, device_id=dev(x, y, (z + k) % 32, c), device_id_type=MESH
        )

    for copy in gz:
        copy.wait_recv()

    g0p = []
    g1p = []
    for k in (2, 1, 3):
        piece = wbuf.at[y, 0:4, c * 4 + x]
        g0p.append(send(piece, piece, g0p_s.at[k - 1], g0p_r.at[k - 1], dev(xp[k], y, z, c)))
        piece = wbuf.at[y, 4:8, c * 4 + x]
        g1p.append(send(piece, piece, g1p_s.at[k - 1], g1p_r.at[k - 1], dev(x, yp[k], z, c)))

    for k in (1, 3, 2):
        a1[k].wait_recv()
    for j in range(4):
        v = ta[x, j].astype(F32)
        for k in range(3):
            v = v + ra[k, j].astype(F32)
        sa[j] = v.astype(BF16)
    a2 = [
        send(sa.at[:, yp[k]], ra2.at[k - 1], a2_s.at[k - 1], a2_r.at[k - 1], dev(x, yp[k], z, c))
        for k in (2, 1, 3)
    ]
    for copy in b1:
        copy.wait_recv()
    for j in range(4):
        v = tb[j, :, y].astype(F32)
        for k in range(3):
            v = v + rb[k, j].astype(F32)
        sb[j] = v.astype(BF16)
    b2 = [
        send(sb.at[xp[k]], rb2.at[k - 1], b2_s.at[k - 1], b2_r.at[k - 1], dev(xp[k], y, z, c))
        for k in (2, 1, 3)
    ]
    forwards = []

    def forward(piece):
        n = len(forwards)
        forwards.append(send(piece, piece, fw_s.at[n], fw_r.at[n], partner))

    for copy in g0p:
        copy.wait_recv()
    g0q = {}
    for k in (2, 1, 3):
        piece = wbuf.at[y, 0:4, pl.ds(c * 4, 4)]
        g0q[k] = send(piece, piece, g0q_s.at[k - 1], g0q_r.at[k - 1], dev(x, yp[k], z, c))
    for copy in g1p:
        copy.wait_recv()
    g1q = {}
    for k in (2, 1, 3):
        piece = wbuf.at[:, 4:8, c * 4 + x]
        g1q[k] = send(piece, piece, g1q_s.at[k - 1], g1q_r.at[k - 1], dev(xp[k], y, z, c))
    forward(wbuf.at[y, 0:4, pl.ds(c * 4, 4)])
    forward(wbuf.at[:, 4:8, c * 4 + x])

    for copy in a2:
        copy.wait_recv()
    for copy in b2:
        copy.wait_recv()
    fa = sa[:, y].astype(F32)
    fb = sb[x].astype(F32)
    for k in range(3):
        fa = fa + ra2[k].astype(F32)
        fb = fb + rb2[k].astype(F32)
    both = jnp.concatenate([fa.reshape(8, 4, 8, 128), fb.reshape(8, 4, 8, 128)], axis=2)
    zbuf[...] = both.astype(BF16)
    za = [
        send(
            zbuf.at[:, (zm + k) % 4], rza.at[k - 1], za_s.at[k - 1], za_r.at[k - 1],
            dev(x, y, zg * 4 + (zm + k) % 4, c),
        )
        for k in (1, 2, 3)
    ]

    for copy in za:
        copy.wait_recv()
    v = zbuf[:, zm].astype(F32)
    for k in range(3):
        v = v + rza[k].astype(F32)
    zb2[...] = v.astype(BF16)
    pl.semaphore_wait(far_s.at[1], 2)
    zb = []
    for k in (4, 3, 5, 2, 6, 1, 7):
        gt = (zg + k) % 8
        zb.append(
            send(zb2.at[gt], rzb.at[k - 1], zb_s.at[k - 1], zb_r.at[k - 1], dev(x, y, gt * 4 + zm, c))
        )

    for k in (1, 3, 2):
        g0q[k].wait_recv()
        forward(wbuf.at[yp[4 - k], 0:4, pl.ds(c * 4, 4)])
        g1q[k].wait_recv()
        forward(wbuf.at[:, 4:8, c * 4 + xp[4 - k]])

    acc[...] = jnp.zeros_like(acc)
    dots = jnp.zeros((TOK, 128), F32)
    for half in range(2):
        for copy in forwards[half::2]:
            copy.wait_recv()

        def block(j, dots, half=half):
            for i in (2 * half, 2 * half + 1):
                rows = slice(i * 256, (i + 1) * 256)
                w = wbuf[j, i * 2:(i + 1) * 2].reshape(256, KW)
                acc[...] += jnp.dot(nrm[j, :, rows], w, preferred_element_type=F32)
                cols = pl.ds(pl.multiple_of(j * 1024 + i * 256, 256), 256)
                ng = lax.dot_general(
                    kg_ref[...], w, (((1,), (1,)), ((), ())), preferred_element_type=F32
                )
                s = ng * gain_ref[:, cols]
                sg[j, :, rows] = s
                p = s * (tok_ref[:, cols].astype(F32) * inv[...])
                dots = dots + p[:, :128] + p[:, 128:]
            return dots

        dots = lax.fori_loop(0, 4, block, dots)
    keys_ref[...] = acc[...].astype(BF16)
    centre = jnp.sum(dots, axis=-1, keepdims=True) * (1.0 / D)

    def finish(j, carry):
        cols = pl.ds(pl.multiple_of(j * 1024, 1024), 1024)
        unit = tok_ref[:, cols].astype(F32) * inv[...]
        ig_ref[:, cols] = ((sg[j] - unit * centre) * inv[...]).astype(BF16)
        return carry

    lax.fori_loop(0, 4, finish, 0)

    for copy in zb:
        copy.wait_recv()
    v = zb2[zg].astype(F32)
    for k in range(7):
        v = v + rzb[k].astype(F32)
    v = v * (TOKENS ** -0.5)
    low = jnp.concatenate([v[0:4], v[8:12]], axis=0)
    high = jnp.concatenate([v[4:8], v[12:16]], axis=0)
    mine = jnp.where(c == 0, low, high)
    fsend[...] = jnp.where(c == 0, high, low)
    fin = send(fsend, frecv, fin_s.at[0], fin_r.at[0], partner)

    fin.wait_recv()
    other = frecv[...]
    first = jnp.where(c == 0, mine, other)
    second = jnp.where(c == 0, other, mine)
    wg_ref[:, 0:128] = first[0:4]
    wg_ref[:, 128:256] = first[4:8]
    wg_ref[:, 256:384] = second[0:4]
    wg_ref[:, 384:512] = second[4:8]

    for copy in sends:
        copy.wait_send()


def place(keys_in, ig_in, wg_in, keys_out, ig_out, wg_out, keys_buf, ig_buf, wg_buf, sem):
    parts = [(ig_in, ig_buf, ig_out, pl.ds(n * 32, 32)) for n in range(4)]
    parts += [(keys_in, keys_buf, keys_out, pl.ds(0, TOK)), (wg_in, wg_buf, wg_out, pl.ds(0, 4))]
    reads = []
    writes = []
    for n, (src, buf, dst, rows) in enumerate(parts):
        reads.append(pltpu.make_async_copy(src.at[rows], buf.at[rows], sem.at[n]))
        writes.append(pltpu.make_async_copy(buf.at[rows], dst.at[rows], sem.at[6 + n]))
    for copy in reads:
        copy.start()
    for n in range(6):
        reads[n].wait()
        writes[n].start()
    for copy in writes:
        copy.wait()


def shards(tokens, norm_gain, key_weight, key_grad):
    vmem = pl.BlockSpec(memory_space=pltpu.VMEM)
    hbm = pl.BlockSpec(memory_space=pl.ANY)
    pairs = (5, 7, 3, 12, 3, 3, 3, 7, 3, 3, 3, 3, 8, 1)
    sems = []
    for n in pairs:
        sems += [pltpu.SemaphoreType.DMA((n,)), pltpu.SemaphoreType.DMA((n,))]
    shapes = (
        jax.ShapeDtypeStruct((TOK, KW), BF16),
        jax.ShapeDtypeStruct((TOK, D), BF16),
        jax.ShapeDtypeStruct((4, KW), F32),
    )
    results = pl.pallas_call(
        kernel,
        name="key_projection",
        out_shape=shapes,
        in_specs=[hbm] * 4,
        out_specs=(vmem, vmem, vmem),
        scratch_shapes=[
            pltpu.VMEM((TOK, D), BF16),
            pltpu.VMEM((1, D), F32),
            pltpu.VMEM((TOK, KW), BF16),
            pltpu.VMEM((4, TOK, 1024), BF16),
            pltpu.VMEM((4, 2, 1024, TOK), BF16),
            pltpu.VMEM((2, TOK, 256), BF16),
            pltpu.VMEM((TOK, 1), F32),
            pltpu.VMEM((4, 4, 4, 64, 128), BF16),
            pltpu.VMEM((4, 4, 4, 64, 128), BF16),
            pltpu.VMEM((3, 4, 4, 64, 128), BF16),
            pltpu.VMEM((3, 4, 4, 64, 128), BF16),
            pltpu.VMEM((4, 4, 64, 128), BF16),
            pltpu.VMEM((4, 4, 64, 128), BF16),
            pltpu.VMEM((3, 4, 64, 128), BF16),
            pltpu.VMEM((3, 4, 64, 128), BF16),
            pltpu.VMEM((8, 4, 16, 128), BF16),
            pltpu.VMEM((3, 8, 16, 128), BF16),
            pltpu.VMEM((8, 16, 128), BF16),
            pltpu.VMEM((7, 16, 128), BF16),
            pltpu.VMEM((8, 128), F32),
            pltpu.VMEM((8, 128), F32),
            pltpu.VMEM((4, 8, 8, 16, KW), BF16),
            pltpu.VMEM((4, TOK, 1024), F32),
            pltpu.VMEM((TOK, KW), F32),
        ] + sems + [pltpu.SemaphoreType.DMA((4,)), pltpu.SemaphoreType.REGULAR((2,))],
        compiler_params=pltpu.CompilerParams(
            collective_id=0, has_side_effects=True, vmem_limit_bytes=60 * 2**20
        ),
    )(tokens, norm_gain.reshape(1, D), key_weight, key_grad)
    return pl.pallas_call(
        place,
        name="place_results",
        out_shape=shapes,
        in_specs=[hbm] * 3,
        out_specs=(hbm, hbm, hbm),
        scratch_shapes=[
            pltpu.VMEM((TOK, KW), BF16),
            pltpu.VMEM((TOK, D), BF16),
            pltpu.VMEM((4, KW), F32),
            pltpu.SemaphoreType.DMA((12,)),
        ],
        compiler_params=pltpu.CompilerParams(vmem_limit_bytes=60 * 2**20),
    )(*results)


def solution(mesh):
    return jax.shard_map(
        shards,
        mesh=mesh,
        in_specs=(P(("grp", "inner"), None), P(), P("inner", None), P(("grp", "inner"), None)),
        out_specs=(P(("grp", "inner"), None), P(("grp", "inner"), None), P(("grp", "inner"), None)),
        check_vma=False,
    )
```

```python
import functools

import jax
import jax.numpy as jnp
from jax import lax
from jax.experimental import pallas as pl
from jax.experimental.pallas import tpu as pltpu
from jax.sharding import PartitionSpec as P

TOK = 128
D = 4096
KW = 512
TOKENS = 131072
F32 = jnp.float32
BF16 = jnp.bfloat16
MESH = pl.DeviceIdType.MESH
WINDOW = (-4, -3, -2, -1, 1, 2, 3)
Z_NEAR = (1, 2, 3, 4, 28, 29, 30, 31)


def kernel(
    tok_hbm, gain_hbm, w_hbm, kg_hbm, keys_hbm, ig_hbm, wg_ref,
    keys_ref, ig_ref,
    tok_ref, gain_ref, kg_ref, nrm, n2, kg2, inv, ta, tb, ra, rb, sa, sb, ra2, rb2, zbuf, rza, zb2, rzb,
    fsend, frecv, wbuf, sg, acc,
    swap_s, swap_r, gz_s, gz_r, a1_s, a1_r, b1_s, b1_r, a2_s, a2_r, b2_s, b2_r,
    za_s, za_r, zb_s, zb_r, g0p_s, g0p_r, g1p_s, g1p_r, g0q_s, g0q_r, g1q_s, g1q_r,
    fw_s, fw_r, fin_s, fin_r, load_s, far_s, out_s,
):
    grp = lax.axis_index("grp")
    inner = lax.axis_index("inner")
    x = grp // 4
    z = (grp % 4) * 8 + (inner // 2) % 8
    y = inner // 16
    c = inner % 2
    oc = 1 - c
    zl = z % 8
    zg = z // 4
    zm = z % 4

    def dev(px, py, pz, pc):
        return (px * 4 + pz // 8, (py * 8 + pz % 8) * 2 + pc)

    sends = []

    def send(src, dst, s, r, target):
        copy = pltpu.make_async_remote_copy(
            src_ref=src, dst_ref=dst, send_sem=s, recv_sem=r,
            device_id=target, device_id_type=MESH,
        )
        copy.start()
        sends.append(copy)
        return copy

    xp = [(x + k) % 4 for k in range(4)]
    yp = [(y + k) % 4 for k in range(4)]
    partner = dev(x, y, z, oc)

    barrier = pltpu.get_barrier_semaphore()
    peers = [partner]
    peers += [dev(xp[k], y, z, c) for k in (1, 2, 3)]
    peers += [dev(x, yp[k], z, c) for k in (1, 2, 3)]
    peers += [dev(x, y, (z + k) % 32, c) for k in Z_NEAR]
    for peer in peers:
        pl.semaphore_signal(barrier, inc=1, device_id=peer, device_id_type=MESH)

    w_own = w_hbm.at[pl.ds(pl.multiple_of(x * 16, 16), 16), :]
    loads = [
        pltpu.make_async_copy(src, dst, load_s.at[n])
        for n, (src, dst) in enumerate(
            (
                (tok_hbm, tok_ref), (gain_hbm, gain_ref), (kg_hbm, kg_ref),
                (w_own, wbuf.at[y, zl, c * 4 + x]),
            )
        )
    ]
    for copy in loads:
        copy.start()
    for copy in loads:
        copy.wait()
    kg2[c] = kg_ref[:, pl.ds(pl.multiple_of(c * 256, 256), 256)]
    total = jnp.zeros((TOK, 128), F32)
    for j in range(D // 512):
        v = tok_ref[:, j * 512:(j + 1) * 512].astype(F32)
        v = v * v
        for i in range(4):
            total = total + v[:, i * 128:(i + 1) * 128]
    inverse = lax.rsqrt(jnp.sum(total, axis=-1, keepdims=True) * (1.0 / D) + 1e-05)
    inv[...] = inverse
    order = (2, 1, 3, 0)
    swaps = {}

    def norm_block(k):
        cols = pl.ds(pl.multiple_of(xp[k] * 1024, 1024), 1024)
        v = tok_ref[:, cols].astype(F32) * inverse
        v = (v * gain_ref[:, cols]).astype(BF16)
        nrm[xp[k]] = v
        n2[xp[k], c] = v.T

    def swap_block(k):
        piece = n2.at[xp[k], c]
        swaps[k] = send(piece, piece, swap_s.at[k], swap_r.at[k], partner)

    norm_block(order[0])
    pl.semaphore_wait(barrier, len(peers))
    kg_copy = send(
        kg_ref.at[:, pl.ds(pl.multiple_of(oc * 256, 256), 256)], kg2.at[c],
        swap_s.at[4], swap_r.at[4], partner,
    )
    swap_block(order[0])

    gz = []
    for n, k in enumerate(WINDOW):
        gz.append(
            send(
                w_own, wbuf.at[y, zl, c * 4 + x], gz_s.at[n], gz_r.at[n],
                dev(x, y, (z + k) % 32, c),
            )
        )

    for k in (4, 28):
        pl.semaphore_signal(
            far_s.at[0], inc=1, device_id=dev(x, y, (z + k) % 32, c), device_id_type=MESH
        )

    for k in order[1:]:
        norm_block(k)
        swap_block(k)

    kg_copy.wait_recv()
    a1, b1 = {}, []
    for k in order:
        swaps[k].wait_recv()
        xt = xp[k]
        for j in range(4):
            rows = slice(j * 256, (j + 1) * 256)
            lhs = jnp.concatenate([n2[xt, 0, rows], n2[xt, 1, rows]], axis=1)
            t = jnp.dot(
                lhs, kg2[...].reshape(2 * TOK, 256), preferred_element_type=F32
            ).astype(BF16)
            ta[xt, j] = t[:, :128].reshape(4, 64, 128)
            tb[xt, j] = t[:, 128:].reshape(4, 64, 128)
        if k:
            a1[k] = send(ta.at[xt], ra.at[k - 1], a1_s.at[k - 1], a1_r.at[k - 1], dev(xt, y, z, c))
        for i in (2, 1, 3):
            n = k * 3 + i - 1
            b1.append(
                send(
                    tb.at[xt, :, yp[i]], rb.at[i - 1, (x + k) % 4], b1_s.at[n], b1_r.at[n],
                    dev(x, yp[i], z, c),
                )
            )
    pl.semaphore_wait(far_s.at[0], 2)
    for k in (8, 24):
        pl.semaphore_signal(
            far_s.at[1], inc=1, device_id=dev(x, y, (z + k) % 32, c), device_id_type=MESH
        )

    for copy in gz:
        copy.wait_recv()

    g0p = []
    g1p = []
    for k in (2, 1, 3):
        piece = wbuf.at[y, 0:4, c * 4 + x]
        g0p.append(send(piece, piece, g0p_s.at[k - 1], g0p_r.at[k - 1], dev(xp[k], y, z, c)))
        piece = wbuf.at[y, 4:8, c * 4 + x]
        g1p.append(send(piece, piece, g1p_s.at[k - 1], g1p_r.at[k - 1], dev(x, yp[k], z, c)))

    for k in (1, 3, 2):
        a1[k].wait_recv()
    for j in range(4):
        v = ta[x, j].astype(F32)
        for k in range(3):
            v = v + ra[k, j].astype(F32)
        sa[j] = v.astype(BF16)
    a2 = [
        send(sa.at[:, yp[k]], ra2.at[k - 1], a2_s.at[k - 1], a2_r.at[k - 1], dev(x, yp[k], z, c))
        for k in (2, 1, 3)
    ]
    for copy in b1:
        copy.wait_recv()
    for j in range(4):
        v = tb[j, :, y].astype(F32)
        for k in range(3):
            v = v + rb[k, j].astype(F32)
        sb[j] = v.astype(BF16)
    b2 = [
        send(sb.at[xp[k]], rb2.at[k - 1], b2_s.at[k - 1], b2_r.at[k - 1], dev(xp[k], y, z, c))
        for k in (2, 1, 3)
    ]
    forwards = []

    def forward(piece):
        n = len(forwards)
        forwards.append(send(piece, piece, fw_s.at[n], fw_r.at[n], partner))

    for copy in g0p + g1p:
        copy.wait_recv()
    g0q, g1q = {}, {}
    for k in (1,):
        piece = wbuf.at[y, 0:4, pl.ds(c * 4, 4)]
        g0q[k] = send(piece, piece, g0q_s.at[k - 1], g0q_r.at[k - 1], dev(x, yp[k], z, c))
        piece = wbuf.at[:, 4:8, c * 4 + x]
        g1q[k] = send(piece, piece, g1q_s.at[k - 1], g1q_r.at[k - 1], dev(xp[k], y, z, c))
    forward(wbuf.at[y, 0:4, pl.ds(c * 4, 4)])
    forward(wbuf.at[:, 4:8, c * 4 + x])

    for copy in a2:
        copy.wait_recv()
    for copy in b2:
        copy.wait_recv()
    fa = sa[:, y].astype(F32)
    fb = sb[x].astype(F32)
    for k in range(3):
        fa = fa + ra2[k].astype(F32)
        fb = fb + rb2[k].astype(F32)
    both = jnp.concatenate([fa.reshape(8, 4, 8, 128), fb.reshape(8, 4, 8, 128)], axis=2)
    zbuf[...] = both.astype(BF16)
    za = [
        send(
            zbuf.at[:, (zm + k) % 4], rza.at[k - 1], za_s.at[k - 1], za_r.at[k - 1],
            dev(x, y, zg * 4 + (zm + k) % 4, c),
        )
        for k in (1, 2, 3)
    ]

    for k in (3, 2):
        piece = wbuf.at[y, 0:4, pl.ds(c * 4, 4)]
        g0q[k] = send(piece, piece, g0q_s.at[k - 1], g0q_r.at[k - 1], dev(x, yp[k], z, c))
        piece = wbuf.at[:, 4:8, c * 4 + x]
        g1q[k] = send(piece, piece, g1q_s.at[k - 1], g1q_r.at[k - 1], dev(xp[k], y, z, c))

    for copy in za:
        copy.wait_recv()
    v = zbuf[:, zm].astype(F32)
    for k in range(3):
        v = v + rza[k].astype(F32)
    zb2[...] = v.astype(BF16)
    pl.semaphore_wait(far_s.at[1], 2)
    zb = []
    for k in (4, 3, 5, 2, 6, 1, 7):
        gt = (zg + k) % 8
        zb.append(
            send(zb2.at[gt], rzb.at[k - 1], zb_s.at[k - 1], zb_r.at[k - 1], dev(x, y, gt * 4 + zm, c))
        )

    for k in (1, 3, 2):
        g0q[k].wait_recv()
        forward(wbuf.at[yp[4 - k], 0:4, pl.ds(c * 4, 4)])
        g1q[k].wait_recv()
        forward(wbuf.at[:, 4:8, c * 4 + xp[4 - k]])

    acc[...] = jnp.zeros_like(acc)
    dots = jnp.zeros((TOK, 128), F32)
    for half in range(2):
        for copy in forwards[half::2]:
            copy.wait_recv()

        def block(j, dots, half=half):
            for i in (2 * half, 2 * half + 1):
                rows = slice(i * 256, (i + 1) * 256)
                w = wbuf[j, i * 2:(i + 1) * 2].reshape(256, KW)
                acc[...] += jnp.dot(nrm[j, :, rows], w, preferred_element_type=F32)
                cols = pl.ds(pl.multiple_of(j * 1024 + i * 256, 256), 256)
                ng = lax.dot_general(
                    kg_ref[...], w, (((1,), (1,)), ((), ())), preferred_element_type=F32
                )
                s = ng * gain_ref[:, cols]
                sg[j, :, rows] = s
                p = s * (tok_ref[:, cols].astype(F32) * inv[...])
                dots = dots + p[:, :128] + p[:, 128:]
            return dots

        dots = lax.fori_loop(0, 4, block, dots)
    keys_ref[...] = acc[...].astype(BF16)
    centre = jnp.sum(dots, axis=-1, keepdims=True) * (1.0 / D)

    def finish(j, carry):
        cols = pl.ds(pl.multiple_of(j * 1024, 1024), 1024)
        unit = tok_ref[:, cols].astype(F32) * inv[...]
        ig_ref[:, cols] = ((sg[j] - unit * centre) * inv[...]).astype(BF16)
        return carry

    lax.fori_loop(0, 4, finish, 0)
    results = [
        pltpu.make_async_copy(keys_ref, keys_hbm, out_s.at[0]),
        pltpu.make_async_copy(ig_ref, ig_hbm, out_s.at[1]),
    ]
    for copy in results:
        copy.start()

    for copy in zb:
        copy.wait_recv()
    v = zb2[zg].astype(F32)
    for k in range(7):
        v = v + rzb[k].astype(F32)
    v = v * (TOKENS ** -0.5)
    low = jnp.concatenate([v[0:4], v[8:12]], axis=0)
    high = jnp.concatenate([v[4:8], v[12:16]], axis=0)
    mine = jnp.where(c == 0, low, high)
    fsend[...] = jnp.where(c == 0, high, low)
    fin = send(fsend, frecv, fin_s.at[0], fin_r.at[0], partner)

    fin.wait_recv()
    other = frecv[...]
    first = jnp.where(c == 0, mine, other)
    second = jnp.where(c == 0, other, mine)
    wg_ref[:, 0:128] = first[0:4]
    wg_ref[:, 128:256] = first[4:8]
    wg_ref[:, 256:384] = second[0:4]
    wg_ref[:, 384:512] = second[4:8]

    for copy in sends:
        copy.wait_send()
    for copy in results:
        copy.wait()


def place(keys_in, ig_in, wg_in, keys_out, ig_out, wg_out, keys_buf, ig_buf, wg_buf, sem):
    parts = [(ig_in, ig_buf, ig_out, pl.ds(n * 32, 32)) for n in range(4)]
    parts += [(keys_in, keys_buf, keys_out, pl.ds(0, TOK)), (wg_in, wg_buf, wg_out, pl.ds(0, 4))]
    reads = []
    writes = []
    for n, (src, buf, dst, rows) in enumerate(parts):
        reads.append(pltpu.make_async_copy(src.at[rows], buf.at[rows], sem.at[n]))
        writes.append(pltpu.make_async_copy(buf.at[rows], dst.at[rows], sem.at[6 + n]))
    for copy in reads:
        copy.start()
    for n in range(6):
        reads[n].wait()
        writes[n].start()
    for copy in writes:
        copy.wait()


def shards(tokens, norm_gain, key_weight, key_grad):
    vmem = pl.BlockSpec(memory_space=pltpu.VMEM)
    hbm = pl.BlockSpec(memory_space=pl.ANY)
    pairs = (5, 7, 3, 12, 3, 3, 3, 7, 3, 3, 3, 3, 8, 1)
    sems = []
    for n in pairs:
        sems += [pltpu.SemaphoreType.DMA((n,)), pltpu.SemaphoreType.DMA((n,))]
    shapes = (
        jax.ShapeDtypeStruct((TOK, KW), BF16),
        jax.ShapeDtypeStruct((TOK, D), BF16),
        jax.ShapeDtypeStruct((4, KW), F32),
    )
    results = pl.pallas_call(
        kernel,
        name="key_projection",
        out_shape=shapes,
        in_specs=[hbm] * 4,
        out_specs=(hbm, hbm, vmem),
        scratch_shapes=[
            pltpu.VMEM((TOK, KW), BF16),
            pltpu.VMEM((TOK, D), BF16),
            pltpu.VMEM((TOK, D), BF16),
            pltpu.VMEM((1, D), F32),
            pltpu.VMEM((TOK, KW), BF16),
            pltpu.VMEM((4, TOK, 1024), BF16),
            pltpu.VMEM((4, 2, 1024, TOK), BF16),
            pltpu.VMEM((2, TOK, 256), BF16),
            pltpu.VMEM((TOK, 1), F32),
            pltpu.VMEM((4, 4, 4, 64, 128), BF16),
            pltpu.VMEM((4, 4, 4, 64, 128), BF16),
            pltpu.VMEM((3, 4, 4, 64, 128), BF16),
            pltpu.VMEM((3, 4, 4, 64, 128), BF16),
            pltpu.VMEM((4, 4, 64, 128), BF16),
            pltpu.VMEM((4, 4, 64, 128), BF16),
            pltpu.VMEM((3, 4, 64, 128), BF16),
            pltpu.VMEM((3, 4, 64, 128), BF16),
            pltpu.VMEM((8, 4, 16, 128), BF16),
            pltpu.VMEM((3, 8, 16, 128), BF16),
            pltpu.VMEM((8, 16, 128), BF16),
            pltpu.VMEM((7, 16, 128), BF16),
            pltpu.VMEM((8, 128), F32),
            pltpu.VMEM((8, 128), F32),
            pltpu.VMEM((4, 8, 8, 16, KW), BF16),
            pltpu.VMEM((4, TOK, 1024), F32),
            pltpu.VMEM((TOK, KW), F32),
        ] + sems + [pltpu.SemaphoreType.DMA((4,)), pltpu.SemaphoreType.REGULAR((2,))]
        + [pltpu.SemaphoreType.DMA((2,))],
        compiler_params=pltpu.CompilerParams(
            collective_id=0, has_side_effects=True, vmem_limit_bytes=60 * 2**20
        ),
    )(tokens, norm_gain.reshape(1, D), key_weight, key_grad)
    return pl.pallas_call(
        place,
        name="place_results",
        out_shape=shapes,
        in_specs=[hbm] * 3,
        out_specs=(hbm, hbm, hbm),
        scratch_shapes=[
            pltpu.VMEM((TOK, KW), BF16),
            pltpu.VMEM((TOK, D), BF16),
            pltpu.VMEM((4, KW), F32),
            pltpu.SemaphoreType.DMA((12,)),
        ],
        compiler_params=pltpu.CompilerParams(vmem_limit_bytes=60 * 2**20),
    )(*results)


def solution(mesh):
    return jax.shard_map(
        shards,
        mesh=mesh,
        in_specs=(P(("grp", "inner"), None), P(), P("inner", None), P(("grp", "inner"), None)),
        out_specs=(P(("grp", "inner"), None), P(("grp", "inner"), None), P(("grp", "inner"), None)),
        check_vma=False,
    )
```

```python
import functools

import jax
import jax.numpy as jnp
from jax import lax
from jax.experimental import pallas as pl
from jax.experimental.pallas import tpu as pltpu
from jax.sharding import PartitionSpec as P

TOK = 128
D = 4096
KW = 512
TOKENS = 131072
F32 = jnp.float32
BF16 = jnp.bfloat16
MESH = pl.DeviceIdType.MESH
WINDOW = (-4, -3, -2, -1, 1, 2, 3)
Z_NEAR = (1, 2, 3, 4, 28, 29, 30, 31)


def kernel(
    tok_hbm, gain_hbm, w_hbm, kg_hbm, keys_hbm, ig_hbm, wg_ref,
    keys_ref, ig_ref,
    tok_ref, gain_ref, kg_ref, nrm, n2, n2_out, kg2, inv, ta, tb, ra, rb, sa, sb, ra2, rb2, zbuf, rza, zb2, rzb,
    wbuf, sg, acc,
    swap_s, swap_r, gz_s, gz_r, a1_s, a1_r, b1_s, b1_r, a2_s, a2_r, b2_s, b2_r,
    za_s, za_r, zb_s, zb_r, g0p_s, g0p_r, g1p_s, g1p_r, g0q_s, g0q_r, g1q_s, g1q_r,
    fw_s, fw_r, load_s, far_s, out_s,
):
    grp = lax.axis_index("grp")
    inner = lax.axis_index("inner")
    x = grp // 4
    z = (grp % 4) * 8 + (inner // 2) % 8
    y = inner // 16
    c = inner % 2
    oc = 1 - c
    zl = z % 8
    zg = z // 4
    zm = z % 4

    def dev(px, py, pz, pc):
        return (px * 4 + pz // 8, (py * 8 + pz % 8) * 2 + pc)

    sends = []

    def send(src, dst, s, r, target):
        copy = pltpu.make_async_remote_copy(
            src_ref=src, dst_ref=dst, send_sem=s, recv_sem=r,
            device_id=target, device_id_type=MESH,
        )
        copy.start()
        sends.append(copy)
        return copy

    xp = [(x + k) % 4 for k in range(4)]
    yp = [(y + k) % 4 for k in range(4)]
    partner = dev(x, y, z, oc)

    barrier = pltpu.get_barrier_semaphore()
    peers = [partner]
    peers += [dev(xp[k], y, z, c) for k in (1, 2, 3)]
    peers += [dev(x, yp[k], z, c) for k in (1, 2, 3)]
    peers += [dev(x, y, (z + k) % 32, c) for k in Z_NEAR]
    for peer in peers:
        pl.semaphore_signal(barrier, inc=1, device_id=peer, device_id_type=MESH)

    w_own = w_hbm.at[pl.ds(pl.multiple_of(x * 16, 16), 16), :]
    loads = [
        pltpu.make_async_copy(src, dst, load_s.at[n])
        for n, (src, dst) in enumerate(
            (
                *(
                    (tok_hbm.at[:, pl.ds(j * 1024, 1024)], tok_ref.at[:, pl.ds(j * 1024, 1024)])
                    for j in range(4)
                ),
                (kg_hbm, kg_ref), (gain_hbm, gain_ref), (w_own, wbuf.at[y, zl, c * 4 + x]),
            )
        )
    ]
    for copy in loads:
        copy.start()
    total = jnp.zeros((TOK, 128), F32)
    for j in range(4):
        loads[j].wait()
        for i in range(8):
            v = tok_ref[:, j * 1024 + i * 128:j * 1024 + (i + 1) * 128].astype(F32)
            total = total + v * v
    for copy in loads[4:]:
        copy.wait()
    kg2[c] = kg_ref[...]
    inverse = lax.rsqrt(jnp.sum(total, axis=-1, keepdims=True) * (1.0 / D) + 1e-05)
    inv[...] = inverse
    order = (2, 1, 3, 0)
    swaps = {}

    row = lax.broadcasted_iota(jnp.int32, (128, 256), 0)
    feature = lax.broadcasted_iota(jnp.int32, (128, 256), 1)
    first = (row // 4) * 8 + row % 4
    own_rows = jnp.where(feature == first + c * 4, 1.0, 0.0).astype(BF16)
    other_rows = jnp.where(feature == first + oc * 4, 1.0, 0.0).astype(BF16)

    def picked(rows, v):
        return lax.dot_general(
            rows, v, (((1,), (1,)), ((), ())), preferred_element_type=F32
        ).astype(BF16)

    def norm_block(k):
        cols = pl.ds(pl.multiple_of(xp[k] * 1024, 1024), 1024)
        v = tok_ref[:, cols].astype(F32) * inverse
        v = (v * gain_ref[:, cols]).astype(BF16)
        nrm[xp[k]] = v
        for j in range(4):
            part = v[:, j * 256:(j + 1) * 256]
            n2_out[xp[k], j * 128:(j + 1) * 128] = picked(other_rows, part)
            n2[xp[k], c, j * 128:(j + 1) * 128] = picked(own_rows, part)

    def swap_block(k):
        swaps[k] = send(n2_out.at[xp[k]], n2.at[xp[k], c], swap_s.at[k], swap_r.at[k], partner)

    norm_block(order[0])
    pl.semaphore_wait(barrier, len(peers))
    kg_copy = send(
        kg_ref, kg2.at[c], swap_s.at[4], swap_r.at[4], partner,
    )
    swap_block(order[0])

    gz = []
    for n, k in enumerate(WINDOW):
        gz.append(
            send(
                w_own, wbuf.at[y, zl, c * 4 + x], gz_s.at[n], gz_r.at[n],
                dev(x, y, (z + k) % 32, c),
            )
        )

    for k in (4, 28):
        pl.semaphore_signal(
            far_s.at[0], inc=1, device_id=dev(x, y, (z + k) % 32, c), device_id_type=MESH
        )

    norm_block(order[1])
    swap_block(order[1])

    kg_copy.wait_recv()
    a1, b1 = {}, []
    for step, k in enumerate(order):
        swaps[k].wait_recv()
        xt = xp[k]
        for j in range(4):
            rows = slice(j * 128, (j + 1) * 128)
            lhs = jnp.concatenate([n2[xt, 0, rows], n2[xt, 1, rows]], axis=1)
            t = jnp.dot(
                lhs, kg2[...].reshape(2 * TOK, KW), preferred_element_type=F32
            ).astype(BF16)
            ta[xt, j] = t[:, :256].reshape(4, 32, 256)
            tb[xt, j] = t[:, 256:].reshape(4, 32, 256)
        if k:
            a1[k] = send(ta.at[xt], ra.at[k - 1], a1_s.at[k - 1], a1_r.at[k - 1], dev(xt, y, z, c))
        for i in (2, 1, 3):
            n = k * 3 + i - 1
            b1.append(
                send(
                    tb.at[xt, :, yp[i]], rb.at[i - 1, (x + k) % 4], b1_s.at[n], b1_r.at[n],
                    dev(x, yp[i], z, c),
                )
            )
        if step + 2 < 4:
            norm_block(order[step + 2])
            swap_block(order[step + 2])
    pl.semaphore_wait(far_s.at[0], 2)
    for k in (8, 24):
        pl.semaphore_signal(
            far_s.at[1], inc=1, device_id=dev(x, y, (z + k) % 32, c), device_id_type=MESH
        )

    for copy in gz:
        copy.wait_recv()

    g0p = []
    g1p = []
    for k in (2, 1, 3):
        piece = wbuf.at[y, 0:4, c * 4 + x]
        g0p.append(send(piece, piece, g0p_s.at[k - 1], g0p_r.at[k - 1], dev(xp[k], y, z, c)))
        piece = wbuf.at[y, 4:8, c * 4 + x]
        g1p.append(send(piece, piece, g1p_s.at[k - 1], g1p_r.at[k - 1], dev(x, yp[k], z, c)))

    for k in (1, 3, 2):
        a1[k].wait_recv()
    for j in range(4):
        v = ta[x, j].astype(F32)
        for k in range(3):
            v = v + ra[k, j].astype(F32)
        sa[j] = v.astype(BF16)
    a2 = [
        send(sa.at[:, yp[k]], ra2.at[k - 1], a2_s.at[k - 1], a2_r.at[k - 1], dev(x, yp[k], z, c))
        for k in (2, 1, 3)
    ]
    for copy in b1:
        copy.wait_recv()
    for j in range(4):
        v = tb[j, :, y].astype(F32)
        for k in range(3):
            v = v + rb[k, j].astype(F32)
        sb[j] = v.astype(BF16)
    b2 = [
        send(sb.at[xp[k]], rb2.at[k - 1], b2_s.at[k - 1], b2_r.at[k - 1], dev(xp[k], y, z, c))
        for k in (2, 1, 3)
    ]
    forwards = []

    def forward(piece):
        n = len(forwards)
        forwards.append(send(piece, piece, fw_s.at[n], fw_r.at[n], partner))

    for copy in g0p + g1p:
        copy.wait_recv()
    g0q, g1q = {}, {}
    for k in (1,):
        piece = wbuf.at[y, 0:4, pl.ds(c * 4, 4)]
        g0q[k] = send(piece, piece, g0q_s.at[k - 1], g0q_r.at[k - 1], dev(x, yp[k], z, c))
        piece = wbuf.at[:, 4:8, c * 4 + x]
        g1q[k] = send(piece, piece, g1q_s.at[k - 1], g1q_r.at[k - 1], dev(xp[k], y, z, c))
    forward(wbuf.at[y, 0:4, pl.ds(c * 4, 4)])
    forward(wbuf.at[:, 4:8, c * 4 + x])

    for copy in a2:
        copy.wait_recv()
    for copy in b2:
        copy.wait_recv()
    fa = sa[:, y].astype(F32)
    fb = sb[x].astype(F32)
    for k in range(3):
        fa = fa + ra2[k].astype(F32)
        fb = fb + rb2[k].astype(F32)
    for zh in range(4):
        for n in range(8):
            four = slice(n * 4, (n + 1) * 4)
            chunk = jnp.concatenate(
                [
                    fa[zh, four, :128], fa[zh, four, 128:],
                    fb[zh, four, :128], fb[zh, four, 128:],
                ],
                axis=0,
            )
            zbuf[zh * 2 + n // 4, n % 4] = chunk.astype(BF16)
    za = [
        send(
            zbuf.at[:, (zm + k) % 4], rza.at[k - 1], za_s.at[k - 1], za_r.at[k - 1],
            dev(x, y, zg * 4 + (zm + k) % 4, c),
        )
        for k in (1, 2, 3)
    ]

    for k in (3, 2):
        piece = wbuf.at[y, 0:4, pl.ds(c * 4, 4)]
        g0q[k] = send(piece, piece, g0q_s.at[k - 1], g0q_r.at[k - 1], dev(x, yp[k], z, c))
        piece = wbuf.at[:, 4:8, c * 4 + x]
        g1q[k] = send(piece, piece, g1q_s.at[k - 1], g1q_r.at[k - 1], dev(xp[k], y, z, c))

    for copy in za:
        copy.wait_recv()
    v = zbuf[:, zm].astype(F32)
    for k in range(3):
        v = v + rza[k].astype(F32)
    zb2[...] = v.astype(BF16)
    pl.semaphore_wait(far_s.at[1], 2)
    zb = []
    for k in (4, 3, 5, 2, 6, 1, 7):
        gt = (zg + k) % 8
        zb.append(
            send(zb2.at[gt], rzb.at[k - 1], zb_s.at[k - 1], zb_r.at[k - 1], dev(x, y, gt * 4 + zm, c))
        )

    acc[...] = jnp.zeros_like(acc)

    def block(j, half, dots):
        for i in (2 * half, 2 * half + 1):
            rows = slice(i * 256, (i + 1) * 256)
            w = wbuf[j, i * 2:(i + 1) * 2].reshape(256, KW)
            acc[...] += jnp.dot(nrm[j, :, rows], w, preferred_element_type=F32)
            cols = pl.ds(pl.multiple_of(j * 1024 + i * 256, 256), 256)
            ng = lax.dot_general(
                kg_ref[...], w, (((1,), (1,)), ((), ())), preferred_element_type=F32
            )
            s = ng * gain_ref[:, cols]
            sg[j, :, rows] = s
            p = s * (tok_ref[:, cols].astype(F32) * inv[...])
            dots = dots + p[:, :128] + p[:, 128:]
        return dots

    dots = jnp.zeros((TOK, 128), F32)
    for k in (1, 3, 2):
        g0q[k].wait_recv()
        forward(wbuf.at[yp[4 - k], 0:4, pl.ds(c * 4, 4)])
        g1q[k].wait_recv()
        forward(wbuf.at[:, 4:8, c * 4 + xp[4 - k]])
        if k == 1:
            forwards[0].wait_recv()
            dots = block(y, 0, dots)
        if k == 3:
            forwards[2].wait_recv()
            dots = block(yp[3], 0, dots)
    for n, k in ((4, 3), (6, 2)):
        forwards[n].wait_recv()
        dots = block(yp[4 - k], 0, dots)
    for copy in forwards[1::2]:
        copy.wait_recv()
    dots = lax.fori_loop(0, 4, lambda j, d: block(j, 1, d), dots)
    keys_ref[...] = acc[...].astype(BF16)
    centre = jnp.sum(dots, axis=-1, keepdims=True) * (1.0 / D)

    def finish(j, carry):
        cols = pl.ds(pl.multiple_of(j * 1024, 1024), 1024)
        unit = tok_ref[:, cols].astype(F32) * inv[...]
        ig_ref[:, cols] = ((sg[j] - unit * centre) * inv[...]).astype(BF16)
        return carry

    lax.fori_loop(0, 4, finish, 0)
    results = [
        pltpu.make_async_copy(keys_ref, keys_hbm, out_s.at[0]),
        pltpu.make_async_copy(ig_ref, ig_hbm, out_s.at[1]),
    ]
    for copy in results:
        copy.start()

    for copy in zb:
        copy.wait_recv()
    v = zb2[zg].astype(F32)
    for k in range(7):
        v = v + rzb[k].astype(F32)
    v = v * (TOKENS ** -0.5)
    for n in range(4):
        wg_ref[:, n * 128:(n + 1) * 128] = v[n * 4:(n + 1) * 4]

    for copy in sends:
        copy.wait_send()
    for copy in results:
        copy.wait()


def place(keys_in, ig_in, wg_in, keys_out, ig_out, wg_out, keys_buf, ig_buf, wg_buf, sem):
    parts = [(ig_in, ig_buf, ig_out, pl.ds(n * 32, 32)) for n in range(4)]
    parts += [(keys_in, keys_buf, keys_out, pl.ds(0, TOK)), (wg_in, wg_buf, wg_out, pl.ds(0, 4))]
    reads = []
    writes = []
    for n, (src, buf, dst, rows) in enumerate(parts):
        reads.append(pltpu.make_async_copy(src.at[rows], buf.at[rows], sem.at[n]))
        writes.append(pltpu.make_async_copy(buf.at[rows], dst.at[rows], sem.at[6 + n]))
    for copy in reads:
        copy.start()
    for n in range(6):
        reads[n].wait()
        writes[n].start()
    for copy in writes:
        copy.wait()


def shards(tokens, norm_gain, key_weight, key_grad):
    vmem = pl.BlockSpec(memory_space=pltpu.VMEM)
    hbm = pl.BlockSpec(memory_space=pl.ANY)
    pairs = (5, 7, 3, 12, 3, 3, 3, 7, 3, 3, 3, 3, 8)
    sems = []
    for n in pairs:
        sems += [pltpu.SemaphoreType.DMA((n,)), pltpu.SemaphoreType.DMA((n,))]
    shapes = (
        jax.ShapeDtypeStruct((TOK, KW), BF16),
        jax.ShapeDtypeStruct((TOK, D), BF16),
        jax.ShapeDtypeStruct((4, KW), F32),
    )
    results = pl.pallas_call(
        kernel,
        name="key_projection",
        out_shape=shapes,
        in_specs=[hbm] * 4,
        out_specs=(hbm, hbm, vmem),
        scratch_shapes=[
            pltpu.VMEM((TOK, KW), BF16),
            pltpu.VMEM((TOK, D), BF16),
            pltpu.VMEM((TOK, D), BF16),
            pltpu.VMEM((1, D), F32),
            pltpu.VMEM((TOK, KW), BF16),
            pltpu.VMEM((4, TOK, 1024), BF16),
            pltpu.VMEM((4, 2, 512, TOK), BF16),
            pltpu.VMEM((4, 512, TOK), BF16),
            pltpu.VMEM((2, TOK, KW), BF16),
            pltpu.VMEM((TOK, 1), F32),
            pltpu.VMEM((4, 4, 4, 32, 256), BF16),
            pltpu.VMEM((4, 4, 4, 32, 256), BF16),
            pltpu.VMEM((3, 4, 4, 32, 256), BF16),
            pltpu.VMEM((3, 4, 4, 32, 256), BF16),
            pltpu.VMEM((4, 4, 32, 256), BF16),
            pltpu.VMEM((4, 4, 32, 256), BF16),
            pltpu.VMEM((3, 4, 32, 256), BF16),
            pltpu.VMEM((3, 4, 32, 256), BF16),
            pltpu.VMEM((8, 4, 16, 128), BF16),
            pltpu.VMEM((3, 8, 16, 128), BF16),
            pltpu.VMEM((8, 16, 128), BF16),
            pltpu.VMEM((7, 16, 128), BF16),
            pltpu.VMEM((4, 8, 8, 16, KW), BF16),
            pltpu.VMEM((4, TOK, 1024), F32),
            pltpu.VMEM((TOK, KW), F32),
        ] + sems + [pltpu.SemaphoreType.DMA((7,)), pltpu.SemaphoreType.REGULAR((2,))]
        + [pltpu.SemaphoreType.DMA((2,))],
        compiler_params=pltpu.CompilerParams(
            collective_id=0, has_side_effects=True, vmem_limit_bytes=60 * 2**20
        ),
    )(tokens, norm_gain.reshape(1, D), key_weight, key_grad)
    return pl.pallas_call(
        place,
        name="place_results",
        out_shape=shapes,
        in_specs=[hbm] * 3,
        out_specs=(hbm, hbm, hbm),
        scratch_shapes=[
            pltpu.VMEM((TOK, KW), BF16),
            pltpu.VMEM((TOK, D), BF16),
            pltpu.VMEM((4, KW), F32),
            pltpu.SemaphoreType.DMA((12,)),
        ],
        compiler_params=pltpu.CompilerParams(vmem_limit_bytes=60 * 2**20),
    )(*results)


def solution(mesh):
    return jax.shard_map(
        shards,
        mesh=mesh,
        in_specs=(P(("grp", "inner"), None), P(), P("inner", None), P(("grp", "inner"), None)),
        out_specs=(P(("grp", "inner"), None), P(("grp", "inner"), None), P(("grp", "inner"), None)),
        check_vma=False,
    )
```

```python
import functools

import jax
import jax.numpy as jnp
from jax import lax
from jax.experimental import pallas as pl
from jax.experimental.pallas import tpu as pltpu
from jax.sharding import PartitionSpec as P

TOK = 128
D = 4096
KW = 512
TOKENS = 131072
F32 = jnp.float32
BF16 = jnp.bfloat16
MESH = pl.DeviceIdType.MESH
WINDOW = (-4, -3, -2, -1, 1, 2, 3)
Z_NEAR = (1, 2, 30, 31)


def kernel(
    tok_hbm, gain_hbm, w_hbm, kg_hbm, keys_hbm, ig_hbm, wg_ref,
    keys_ref, ig_ref,
    tok_ref, gain_ref, kg_ref, nrm, n2, n2_out, kg2, inv, ta, tb, ra, rb, sa, sb, ra2, rb2, zbuf, rza, zb2, rzb,
    wbuf, sg, acc,
    swap_s, swap_r, gz_s, gz_r, a1_s, a1_r, b1_s, b1_r, a2_s, a2_r, b2_s, b2_r,
    za_s, za_r, zb_s, zb_r, g0p_s, g0p_r, g1p_s, g1p_r, g0q_s, g0q_r, g1q_s, g1q_r,
    fw_s, fw_r, load_s, far_s, out_s,
):
    grp = lax.axis_index("grp")
    inner = lax.axis_index("inner")
    x = grp // 4
    z = (grp % 4) * 8 + (inner // 2) % 8
    y = inner // 16
    c = inner % 2
    oc = 1 - c
    zl = z % 8
    zg = z // 4
    zm = z % 4

    def dev(px, py, pz, pc):
        return (px * 4 + pz // 8, (py * 8 + pz % 8) * 2 + pc)

    sends = []

    def send(src, dst, s, r, target):
        copy = pltpu.make_async_remote_copy(
            src_ref=src, dst_ref=dst, send_sem=s, recv_sem=r,
            device_id=target, device_id_type=MESH,
        )
        copy.start()
        sends.append(copy)
        return copy

    xp = [(x + k) % 4 for k in range(4)]
    yp = [(y + k) % 4 for k in range(4)]
    partner = dev(x, y, z, oc)

    barrier = pltpu.get_barrier_semaphore()
    peers = [partner]
    peers += [dev(xp[k], y, z, c) for k in (1, 2, 3)]
    peers += [dev(x, yp[k], z, c) for k in (1, 2, 3)]
    peers += [dev(x, y, (z + k) % 32, c) for k in Z_NEAR]
    for peer in peers:
        pl.semaphore_signal(barrier, inc=1, device_id=peer, device_id_type=MESH)

    w_own = w_hbm.at[pl.ds(pl.multiple_of(x * 16, 16), 16), :]
    loads = [
        pltpu.make_async_copy(src, dst, load_s.at[n])
        for n, (src, dst) in enumerate(
            (
                *(
                    (tok_hbm.at[:, pl.ds(j * 1024, 1024)], tok_ref.at[:, pl.ds(j * 1024, 1024)])
                    for j in range(4)
                ),
                (kg_hbm, kg_ref), (gain_hbm, gain_ref), (w_own, wbuf.at[y, zl, c * 4 + x]),
            )
        )
    ]
    for copy in loads:
        copy.start()
    total = jnp.zeros((TOK, 128), F32)
    for j in range(4):
        loads[j].wait()
        for i in range(8):
            v = tok_ref[:, j * 1024 + i * 128:j * 1024 + (i + 1) * 128].astype(F32)
            total = total + v * v
    for copy in loads[4:]:
        copy.wait()
    kg2[c] = kg_ref[...]
    inverse = lax.rsqrt(jnp.sum(total, axis=-1, keepdims=True) * (1.0 / D) + 1e-05)
    inv[...] = inverse
    order = (2, 1, 3, 0)
    swaps = {}

    row = lax.broadcasted_iota(jnp.int32, (128, 256), 0)
    feature = lax.broadcasted_iota(jnp.int32, (128, 256), 1)
    first = (row // 4) * 8 + row % 4
    own_rows = jnp.where(feature == first + c * 4, 1.0, 0.0).astype(BF16)
    other_rows = jnp.where(feature == first + oc * 4, 1.0, 0.0).astype(BF16)

    def picked(rows, v):
        return lax.dot_general(
            rows, v, (((1,), (1,)), ((), ())), preferred_element_type=F32
        ).astype(BF16)

    def norm_block(k):
        cols = pl.ds(pl.multiple_of(xp[k] * 1024, 1024), 1024)
        v = tok_ref[:, cols].astype(F32) * inverse
        v = (v * gain_ref[:, cols]).astype(BF16)
        nrm[xp[k]] = v
        for j in range(4):
            part = v[:, j * 256:(j + 1) * 256]
            n2_out[xp[k], j * 128:(j + 1) * 128] = picked(other_rows, part)
            n2[xp[k], c, j * 128:(j + 1) * 128] = picked(own_rows, part)

    def swap_block(k):
        swaps[k] = send(n2_out.at[xp[k]], n2.at[xp[k], c], swap_s.at[k], swap_r.at[k], partner)

    norm_block(order[0])
    pl.semaphore_wait(barrier, len(peers))
    kg_copy = send(
        kg_ref, kg2.at[c], swap_s.at[4], swap_r.at[4], partner,
    )
    swap_block(order[0])

    for k in (2, 30):
        pl.semaphore_signal(
            far_s.at[0], inc=1, device_id=dev(x, y, (z + k) % 32, c), device_id_type=MESH
        )

    norm_block(order[1])
    swap_block(order[1])

    kg_copy.wait_recv()
    a1, b1 = {}, []
    for step, k in enumerate(order):
        swaps[k].wait_recv()
        xt = xp[k]
        for j in range(4):
            rows = slice(j * 128, (j + 1) * 128)
            lhs = jnp.concatenate([n2[xt, 0, rows], n2[xt, 1, rows]], axis=1)
            t = jnp.dot(
                lhs, kg2[...].reshape(2 * TOK, KW), preferred_element_type=F32
            ).astype(BF16)
            ta[xt, j] = t[:, :256].reshape(4, 32, 256)
            tb[xt, j] = t[:, 256:].reshape(4, 32, 256)
        if k:
            a1[k] = send(ta.at[xt], ra.at[k - 1], a1_s.at[k - 1], a1_r.at[k - 1], dev(xt, y, z, c))
        for i in (2, 1, 3):
            n = k * 3 + i - 1
            b1.append(
                send(
                    tb.at[xt, :, yp[i]], rb.at[i - 1, (x + k) % 4], b1_s.at[n], b1_r.at[n],
                    dev(x, yp[i], z, c),
                )
            )
        if step == 0:
            pl.semaphore_wait(far_s.at[0], 2)
            for k4 in (4, 28):
                pl.semaphore_signal(
                    far_s.at[1], inc=1, device_id=dev(x, y, (z + k4) % 32, c), device_id_type=MESH
                )

            gz = []
            for n, far in enumerate(WINDOW):
                gz.append(
                    send(
                        w_own, wbuf.at[y, zl, c * 4 + x], gz_s.at[n], gz_r.at[n],
                        dev(x, y, (z + far) % 32, c),
                    )
                )
        if step + 2 < 4:
            norm_block(order[step + 2])
            swap_block(order[step + 2])
    pl.semaphore_wait(far_s.at[1], 2)
    for k in (8, 24):
        pl.semaphore_signal(
            far_s.at[2], inc=1, device_id=dev(x, y, (z + k) % 32, c), device_id_type=MESH
        )

    for copy in gz:
        copy.wait_recv()

    g0p = []
    g1p = []
    for k in (2, 1, 3):
        piece = wbuf.at[y, 0:4, c * 4 + x]
        g0p.append(send(piece, piece, g0p_s.at[k - 1], g0p_r.at[k - 1], dev(xp[k], y, z, c)))
        piece = wbuf.at[y, 4:8, c * 4 + x]
        g1p.append(send(piece, piece, g1p_s.at[k - 1], g1p_r.at[k - 1], dev(x, yp[k], z, c)))

    for k in (1, 3, 2):
        a1[k].wait_recv()
    for j in range(4):
        v = ta[x, j].astype(F32)
        for k in range(3):
            v = v + ra[k, j].astype(F32)
        sa[j] = v.astype(BF16)
    a2 = [
        send(sa.at[:, yp[k]], ra2.at[k - 1], a2_s.at[k - 1], a2_r.at[k - 1], dev(x, yp[k], z, c))
        for k in (2, 1, 3)
    ]
    for copy in b1:
        copy.wait_recv()
    for j in range(4):
        v = tb[j, :, y].astype(F32)
        for k in range(3):
            v = v + rb[k, j].astype(F32)
        sb[j] = v.astype(BF16)
    b2 = [
        send(sb.at[xp[k]], rb2.at[k - 1], b2_s.at[k - 1], b2_r.at[k - 1], dev(xp[k], y, z, c))
        for k in (2, 1, 3)
    ]
    forwards = []

    def forward(piece):
        n = len(forwards)
        forwards.append(send(piece, piece, fw_s.at[n], fw_r.at[n], partner))

    for copy in g0p + g1p:
        copy.wait_recv()
    g0q, g1q = {}, {}
    for k in (1,):
        piece = wbuf.at[y, 0:4, pl.ds(c * 4, 4)]
        g0q[k] = send(piece, piece, g0q_s.at[k - 1], g0q_r.at[k - 1], dev(x, yp[k], z, c))
        piece = wbuf.at[:, 4:8, c * 4 + x]
        g1q[k] = send(piece, piece, g1q_s.at[k - 1], g1q_r.at[k - 1], dev(xp[k], y, z, c))
    forward(wbuf.at[y, 0:4, pl.ds(c * 4, 4)])
    forward(wbuf.at[:, 4:8, c * 4 + x])

    for copy in a2:
        copy.wait_recv()
    for copy in b2:
        copy.wait_recv()
    fa = sa[:, y].astype(F32)
    fb = sb[x].astype(F32)
    for k in range(3):
        fa = fa + ra2[k].astype(F32)
        fb = fb + rb2[k].astype(F32)
    for zh in range(4):
        for n in range(8):
            four = slice(n * 4, (n + 1) * 4)
            chunk = jnp.concatenate(
                [
                    fa[zh, four, :128], fa[zh, four, 128:],
                    fb[zh, four, :128], fb[zh, four, 128:],
                ],
                axis=0,
            )
            zbuf[zh * 2 + n // 4, n % 4] = chunk.astype(BF16)
    za = [
        send(
            zbuf.at[:, (zm + k) % 4], rza.at[k - 1], za_s.at[k - 1], za_r.at[k - 1],
            dev(x, y, zg * 4 + (zm + k) % 4, c),
        )
        for k in (1, 2, 3)
    ]

    for k in (3, 2):
        piece = wbuf.at[y, 0:4, pl.ds(c * 4, 4)]
        g0q[k] = send(piece, piece, g0q_s.at[k - 1], g0q_r.at[k - 1], dev(x, yp[k], z, c))
        piece = wbuf.at[:, 4:8, c * 4 + x]
        g1q[k] = send(piece, piece, g1q_s.at[k - 1], g1q_r.at[k - 1], dev(xp[k], y, z, c))

    for copy in za:
        copy.wait_recv()
    v = zbuf[:, zm].astype(F32)
    for k in range(3):
        v = v + rza[k].astype(F32)
    zb2[...] = v.astype(BF16)
    pl.semaphore_wait(far_s.at[2], 2)
    zb = []
    for k in (4, 3, 5, 2, 6, 1, 7):
        gt = (zg + k) % 8
        zb.append(
            send(zb2.at[gt], rzb.at[k - 1], zb_s.at[k - 1], zb_r.at[k - 1], dev(x, y, gt * 4 + zm, c))
        )

    acc[...] = jnp.zeros_like(acc)

    def block(j, half, dots):
        for i in (2 * half, 2 * half + 1):
            rows = slice(i * 256, (i + 1) * 256)
            w = wbuf[j, i * 2:(i + 1) * 2].reshape(256, KW)
            acc[...] += jnp.dot(nrm[j, :, rows], w, preferred_element_type=F32)
            cols = pl.ds(pl.multiple_of(j * 1024 + i * 256, 256), 256)
            ng = lax.dot_general(
                kg_ref[...], w, (((1,), (1,)), ((), ())), preferred_element_type=F32
            )
            s = ng * gain_ref[:, cols]
            sg[j, :, rows] = s
            p = s * (tok_ref[:, cols].astype(F32) * inv[...])
            dots = dots + p[:, :128] + p[:, 128:]
        return dots

    dots = jnp.zeros((TOK, 128), F32)
    for k in (1, 3, 2):
        g0q[k].wait_recv()
        forward(wbuf.at[yp[4 - k], 0:4, pl.ds(c * 4, 4)])
        g1q[k].wait_recv()
        forward(wbuf.at[:, 4:8, c * 4 + xp[4 - k]])
        if k == 1:
            forwards[0].wait_recv()
            dots = block(y, 0, dots)
        if k == 3:
            forwards[2].wait_recv()
            dots = block(yp[3], 0, dots)
    for n, k in ((4, 3), (6, 2)):
        forwards[n].wait_recv()
        dots = block(yp[4 - k], 0, dots)
    for copy in forwards[1::2]:
        copy.wait_recv()
    dots = lax.fori_loop(0, 4, lambda j, d: block(j, 1, d), dots)
    keys_ref[...] = acc[...].astype(BF16)
    centre = jnp.sum(dots, axis=-1, keepdims=True) * (1.0 / D)

    def finish(j, carry):
        cols = pl.ds(pl.multiple_of(j * 1024, 1024), 1024)
        unit = tok_ref[:, cols].astype(F32) * inv[...]
        ig_ref[:, cols] = ((sg[j] - unit * centre) * inv[...]).astype(BF16)
        return carry

    lax.fori_loop(0, 4, finish, 0)
    results = [
        pltpu.make_async_copy(keys_ref, keys_hbm, out_s.at[0]),
        pltpu.make_async_copy(ig_ref, ig_hbm, out_s.at[1]),
    ]
    for copy in results:
        copy.start()

    for copy in zb:
        copy.wait_recv()
    v = zb2[zg].astype(F32)
    for k in range(7):
        v = v + rzb[k].astype(F32)
    v = v * (TOKENS ** -0.5)
    for n in range(4):
        wg_ref[:, n * 128:(n + 1) * 128] = v[n * 4:(n + 1) * 4]

    for copy in sends:
        copy.wait_send()
    for copy in results:
        copy.wait()


def place(keys_in, ig_in, wg_in, keys_out, ig_out, wg_out, keys_buf, ig_buf, wg_buf, sem):
    parts = [(ig_in, ig_buf, ig_out, pl.ds(n * 32, 32)) for n in range(4)]
    parts += [(keys_in, keys_buf, keys_out, pl.ds(0, TOK)), (wg_in, wg_buf, wg_out, pl.ds(0, 4))]
    reads = []
    writes = []
    for n, (src, buf, dst, rows) in enumerate(parts):
        reads.append(pltpu.make_async_copy(src.at[rows], buf.at[rows], sem.at[n]))
        writes.append(pltpu.make_async_copy(buf.at[rows], dst.at[rows], sem.at[6 + n]))
    for copy in reads:
        copy.start()
    for n in range(6):
        reads[n].wait()
        writes[n].start()
    for copy in writes:
        copy.wait()


def shards(tokens, norm_gain, key_weight, key_grad):
    vmem = pl.BlockSpec(memory_space=pltpu.VMEM)
    hbm = pl.BlockSpec(memory_space=pl.ANY)
    pairs = (5, 7, 3, 12, 3, 3, 3, 7, 3, 3, 3, 3, 8)
    sems = []
    for n in pairs:
        sems += [pltpu.SemaphoreType.DMA((n,)), pltpu.SemaphoreType.DMA((n,))]
    shapes = (
        jax.ShapeDtypeStruct((TOK, KW), BF16),
        jax.ShapeDtypeStruct((TOK, D), BF16),
        jax.ShapeDtypeStruct((4, KW), F32),
    )
    results = pl.pallas_call(
        kernel,
        name="key_projection",
        out_shape=shapes,
        in_specs=[hbm] * 4,
        out_specs=(hbm, hbm, vmem),
        scratch_shapes=[
            pltpu.VMEM((TOK, KW), BF16),
            pltpu.VMEM((TOK, D), BF16),
            pltpu.VMEM((TOK, D), BF16),
            pltpu.VMEM((1, D), F32),
            pltpu.VMEM((TOK, KW), BF16),
            pltpu.VMEM((4, TOK, 1024), BF16),
            pltpu.VMEM((4, 2, 512, TOK), BF16),
            pltpu.VMEM((4, 512, TOK), BF16),
            pltpu.VMEM((2, TOK, KW), BF16),
            pltpu.VMEM((TOK, 1), F32),
            pltpu.VMEM((4, 4, 4, 32, 256), BF16),
            pltpu.VMEM((4, 4, 4, 32, 256), BF16),
            pltpu.VMEM((3, 4, 4, 32, 256), BF16),
            pltpu.VMEM((3, 4, 4, 32, 256), BF16),
            pltpu.VMEM((4, 4, 32, 256), BF16),
            pltpu.VMEM((4, 4, 32, 256), BF16),
            pltpu.VMEM((3, 4, 32, 256), BF16),
            pltpu.VMEM((3, 4, 32, 256), BF16),
            pltpu.VMEM((8, 4, 16, 128), BF16),
            pltpu.VMEM((3, 8, 16, 128), BF16),
            pltpu.VMEM((8, 16, 128), BF16),
            pltpu.VMEM((7, 16, 128), BF16),
            pltpu.VMEM((4, 8, 8, 16, KW), BF16),
            pltpu.VMEM((4, TOK, 1024), F32),
            pltpu.VMEM((TOK, KW), F32),
        ] + sems + [pltpu.SemaphoreType.DMA((7,)), pltpu.SemaphoreType.REGULAR((3,))]
        + [pltpu.SemaphoreType.DMA((2,))],
        compiler_params=pltpu.CompilerParams(
            collective_id=0, has_side_effects=True, vmem_limit_bytes=60 * 2**20
        ),
    )(tokens, norm_gain.reshape(1, D), key_weight, key_grad)
    return pl.pallas_call(
        place,
        name="place_results",
        out_shape=shapes,
        in_specs=[hbm] * 3,
        out_specs=(hbm, hbm, hbm),
        scratch_shapes=[
            pltpu.VMEM((TOK, KW), BF16),
            pltpu.VMEM((TOK, D), BF16),
            pltpu.VMEM((4, KW), F32),
            pltpu.SemaphoreType.DMA((12,)),
        ],
        compiler_params=pltpu.CompilerParams(vmem_limit_bytes=60 * 2**20),
    )(*results)


def solution(mesh):
    return jax.shard_map(
        shards,
        mesh=mesh,
        in_specs=(P(("grp", "inner"), None), P(), P("inner", None), P(("grp", "inner"), None)),
        out_specs=(P(("grp", "inner"), None), P(("grp", "inner"), None), P(("grp", "inner"), None)),
        check_vma=False,
    )
```
